256 devices in a mesh: chan: 16 (over y, x_hi, core), seg: 16 (over x_lo, z).
Axes of the slice: x: 4 (x_hi: 2, x_lo: 2; x = x_hi * 2 + x_lo), y: 4, z: 8, core: 2. Of those that a mesh axis runs over, the one named last changes fastest.
Arguments:
- samples: bfloat16 [4096, 240, 1024], P('chan', 'seg'), may hold values from -1000 to 1000
- live_trace: int32 [4096], P('chan'), may hold values 0 or 1
Outputs:
- stacked: bfloat16 [64, 4096, 5, 512], P('seg', 'chan')
The draws below stay inside these ranges and needn't reach their ends.
All inputs are finite; a program needn't handle non-finite values. No bound on the sum of `live_trace` on one device may be relied on, other than what follows from the above.
Results may differ from the reference program's by a relative error of at most 0.0057.
Values may be sent and summed in bfloat16 or wider, within the bound.
A program may use at most 64 MiB of HBM per device.

```python
import math
import jax
import jax.numpy as jnp
from jax import lax

CH_DEV = 256
L = 1024
F = 64
F0 = 16
REACH = 4
CHANNELS = 4096
SEGMENTS = 240
NEAR = 5
MAXOFF = 1024
N_CHAN = 16


def draw_samples(key, part):
    key_noise, key_common, key_chan, key_seg, key_block, key_tone = jax.random.split(key, 6)
    chan_pos = jnp.arange(CHANNELS, dtype=jnp.float32) / CHANNELS
    seg_pos = jnp.arange(SEGMENTS, dtype=jnp.float32) / SEGMENTS
    chan_rough = jnp.exp(jax.random.uniform(key_chan, (CHANNELS,), jnp.float32) * math.log(3.0))
    seg_rough = jnp.exp(jax.random.uniform(key_seg, (SEGMENTS,), jnp.float32) * math.log(4.0))
    noise_part = jax.random.truncated_normal(key_noise, -5.0, 5.0, (CHANNELS, SEGMENTS, L), jnp.float32)
    common = jax.random.truncated_normal(key_common, -5.0, 5.0, (SEGMENTS, L), jnp.float32)
    chan_gain = chan_rough * jnp.exp(chan_pos * math.log(3.0))
    common_share = 0.3
    seg_gain = seg_rough * jnp.exp(seg_pos * math.log(3.0))
    block_count = CHANNELS // CH_DEV
    block_gain = jnp.exp(jax.random.uniform(key_block, (block_count, SEGMENTS), jnp.float32) * math.log(3.0))
    cell_gain = jnp.repeat(block_gain, CH_DEV, axis=0)
    key_bin, key_level, key_share, key_phase = jax.random.split(key_tone, 4)
    tone_bins = F0 + jax.random.randint(key_bin, (3,), 0, F)
    tone_level = jnp.exp(jax.random.uniform(key_level, (SEGMENTS, 3), jnp.float32, math.log(0.03), math.log(0.4)))
    tone_share = jax.random.uniform(key_share, (CHANNELS, 3), jnp.float32, 0.5, 1.0)
    tone_phase = jax.random.uniform(key_phase, (CHANNELS, SEGMENTS, 3), jnp.float32, -math.pi, math.pi)
    time_index = jnp.arange(L, dtype=jnp.int32)
    recording = noise_part + common_share * common[None, :, :]
    for tone_number in range(3):
        phase_step = (time_index * tone_bins[tone_number] % L).astype(jnp.float32) * (2.0 * math.pi / L)
        tone_amp = tone_share[:, tone_number][:, None, None] * tone_level[:, tone_number][None, :, None]
        recording = recording + tone_amp * jnp.cos(phase_step[None, None, :] + tone_phase[:, :, tone_number][:, :, None])
    total_gain = 0.25 * chan_gain[:, None] * seg_gain[None, :] * cell_gain
    recording = recording * total_gain[:, :, None]
    return recording.astype(jnp.bfloat16)


def set_ends(array, key, smallest, top_value):
    extent = array.shape
    place = [jax.random.randint(jax.random.fold_in(key, axis), (), 0, extent[axis]) for axis in range(len(extent))]
    array = array.at[tuple(place)].set(smallest)
    longest = extent.index(max(extent))
    place[longest] = (place[longest] + 1) % extent[longest]
    return array.at[tuple(place)].set(top_value)


def setup_inputs(seed: int = 0) -> dict:
    splits = jax.random.split(jax.random.key(seed), 3)
    samples = draw_samples(jax.random.fold_in(splits[2], 71), 0)
    live_trace = set_ends((jax.random.randint(splits[1], (CHANNELS,), 0, 8) < 7).astype(jnp.int32), jax.random.fold_in(splits[1], 1), 0, 1)
    return dict(samples=samples, live_trace=live_trace)


eps_power = 1e-06
water_level = 0.1
smooth_half = 2

def dft_table(length, first, bins):
    sample_index = jnp.arange(length, dtype=jnp.int32)
    bin_number = jnp.arange(bins, dtype=jnp.int32) + first
    phase_step = (sample_index[:, None] * bin_number[None, :] % length).astype(jnp.float32)
    angle_value = phase_step * (2.0 * math.pi / length)
    window_taper = 0.5 - 0.5 * jnp.cos(sample_index.astype(jnp.float32) * (2.0 * math.pi / length))
    stacked_table = jnp.stack([window_taper[:, None] * jnp.cos(angle_value), -window_taper[:, None] * jnp.sin(angle_value)], axis=-1)
    return stacked_table.reshape(length, 2 * bins).astype(jnp.bfloat16)

def smoother(bins):
    bin_index = jnp.arange(bins, dtype=jnp.int32)
    in_window = (jnp.abs(bin_index[:, None] - bin_index[None, :]) <= smooth_half).astype(jnp.float32)
    return in_window / lax.optimization_barrier(jnp.sum(in_window, axis=0, keepdims=True))

def reference(samples, live_trace):
    transform_table = dft_table(L, F0, F)
    alive_mask = live_trace.astype(jnp.float32)
    chan_blocks = samples.reshape(N_CHAN, CH_DEV, SEGMENTS, L)
    alive_blocks = alive_mask.reshape(N_CHAN, CH_DEV)

    def transform(block_pair):
        chan_block, mask_block = block_pair
        block_spectra = jnp.dot(chan_block.reshape(CH_DEV * SEGMENTS, L), transform_table, preferred_element_type=jnp.float32)
        wide_block = chan_block.astype(jnp.float32)
        energy = jnp.einsum('csl,csl->cs', wide_block, wide_block)
        return (block_spectra.reshape(CH_DEV, SEGMENTS, F, 2), lax.optimization_barrier(jnp.sum(mask_block[:, None] * energy, axis=0)))
    spectra, partial_power = lax.map(transform, (chan_blocks, alive_blocks))
    power_sum = lax.optimization_barrier(jnp.sum(partial_power, axis=0))
    weights = 1.0 / jnp.sqrt(power_sum / (CHANNELS * L) + eps_power)
    weight_total = jnp.sum(weights)
    spectra = spectra.reshape(CHANNELS, SEGMENTS, F, 2)
    power_level = spectra[..., 0] * spectra[..., 0] + spectra[..., 1] * spectra[..., 1]
    smooth = jnp.dot(power_level.reshape(CHANNELS * SEGMENTS, F), smoother(F), precision=lax.Precision.HIGHEST).reshape(CHANNELS, SEGMENTS, F)
    denominator = jnp.sqrt(smooth + water_level * lax.optimization_barrier(jnp.mean(power_level, axis=-1, keepdims=True)) + eps_power)
    gain_value = alive_mask[:, None, None] * jnp.sqrt(weights)[None, :, None] / denominator
    whitened = (spectra * gain_value[..., None]).astype(jnp.bfloat16)
    padded = jnp.concatenate([whitened, jnp.zeros((REACH * CH_DEV, SEGMENTS, F, 2), jnp.bfloat16)], axis=0)
    row_index = jnp.arange(CH_DEV, dtype=jnp.int32)
    offsets = jnp.arange(NEAR, dtype=jnp.int32)
    distance = offsets[:, None] * CH_DEV + row_index[None, :]
    distance = distance[None, :, :] - row_index[:, None, None]
    pair_mask = ((distance > 0) & (distance <= MAXOFF)).astype(jnp.float32)
    factor = math.sqrt(SEGMENTS) / weight_total

    def correlate(first_row):
        own_rows = lax.dynamic_slice_in_dim(padded, first_row, CH_DEV, 0).astype(jnp.float32)
        partner_rows = lax.dynamic_slice_in_dim(padded, first_row, NEAR * CH_DEV, 0).astype(jnp.float32)
        real_part = jnp.einsum('csf,msf->fcm', own_rows[..., 0], partner_rows[..., 0]) + jnp.einsum('csf,msf->fcm', own_rows[..., 1], partner_rows[..., 1])
        imag_part = jnp.einsum('csf,msf->fcm', own_rows[..., 0], partner_rows[..., 1]) - jnp.einsum('csf,msf->fcm', own_rows[..., 1], partner_rows[..., 0])
        stacked_parts = jnp.stack([real_part.reshape(F, CH_DEV, NEAR, CH_DEV), imag_part.reshape(F, CH_DEV, NEAR, CH_DEV)], axis=3)
        stacked_parts = stacked_parts * (factor * pair_mask)[None, :, :, None, :]
        return stacked_parts.reshape(F, CH_DEV, NEAR, 2 * CH_DEV).astype(jnp.bfloat16)
    block_starts = jnp.arange(N_CHAN, dtype=jnp.int32) * CH_DEV
    stacked = lax.map(correlate, block_starts)
    return jnp.transpose(stacked, (1, 0, 2, 3, 4)).reshape(F, CHANNELS, NEAR, 2 * CH_DEV)
```

```python
import functools
import math

import jax
import jax.numpy as jnp
import numpy as np
from jax import lax
from jax.experimental import pallas as pl
from jax.experimental.pallas import tpu as pltpu
from jax.sharding import PartitionSpec as P

L = 1024
F = 64
F0 = 16
REACH = 4
NEAR = 5
CH = 256
CHANNELS = 4096
SEGMENTS = 240
N_CHAN = 16
N_SEG = 16
SEG_DEV = 15
SEG_PAD = 16
BAND = F // N_SEG
STEP = 3

eps_power = 1e-06
water_level = 0.1
smooth_half = 2

MESH = pl.DeviceIdType.MESH


def dft_table():
    time_index = np.arange(L)
    bin_number = np.arange(F) + F0
    phase_step = (time_index[:, None] * bin_number[None, :] % L).astype(np.float32)
    angle = phase_step * np.float32(2.0 * math.pi / L)
    taper = np.float32(0.5) - np.float32(0.5) * np.cos(
        time_index.astype(np.float32) * np.float32(2.0 * math.pi / L)
    )
    real = taper[:, None] * np.cos(angle)
    imag = -taper[:, None] * np.sin(angle)
    return np.concatenate([real, imag], axis=1).astype(jnp.bfloat16)


def inverse_counts():
    bins = np.arange(F)
    count = np.minimum(bins, smooth_half) + np.minimum(F - 1 - bins, smooth_half) + 1
    return np.broadcast_to((1.0 / count).astype(np.float32)[:, None], (F, CH)).copy()


def whiten_kernel(x_ref, table_ref, row_ref, col_ref, count_ref, out_ref, power_ref, wide, padded):
    step = pl.program_id(0)
    lane = lax.broadcasted_iota(jnp.int32, (1, 128), 1)

    @pl.when(step == 0)
    def _():
        power_ref[...] = jnp.zeros_like(power_ref)
        padded[...] = jnp.zeros_like(padded)
        for half in range(2):
            wide[half, SEG_DEV * 2 * F :, :] = jnp.zeros((2 * F, 128), jnp.float32)

    for j in range(STEP):
        seg = step * STEP + j
        x = x_ref[j]
        spectra = jnp.dot(x, table_ref[...], preferred_element_type=jnp.float32)
        squares = jnp.zeros((CH, 128), jnp.float32)
        for tile in range(L // 128):
            part = x[:, tile * 128 : (tile + 1) * 128].astype(jnp.float32)
            squares += part * part
        total = jnp.sum(squares * col_ref[...])
        power_ref[...] += jnp.where(lane == seg, total, 0.0)
        spectra = spectra.T
        real = spectra[:F]
        imag = spectra[F:]
        level = real * real + imag * imag
        padded[8 : 8 + F, :] = level
        near = level
        for distance in (-2, -1, 1, 2):
            near += padded[8 + distance : 8 + distance + F, :]
        mean = jnp.sum(level, axis=0, keepdims=True) * (water_level / F)
        gain = row_ref[...] / jnp.sqrt(near * count_ref[...] + mean + eps_power)
        real = real * gain
        imag = imag * gain
        base = pl.multiple_of(seg * 2 * F, 2 * F)
        for half in range(2):
            lanes = slice(half * 128, half * 128 + 128)
            wide[half, pl.ds(base, F), :] = real[:, lanes]
            wide[half, pl.ds(base + F, F), :] = imag[:, lanes]

    @pl.when(step == SEG_DEV // STEP - 1)
    def _():
        for bin_number in range(F):
            for r in range(2):
                for half in range(2):
                    rows = wide[half, pl.ds(r * F + bin_number, SEG_PAD, stride=2 * F), :]
                    out_ref[
                        bin_number // BAND,
                        bin_number % BAND,
                        r * SEG_PAD : (r + 1) * SEG_PAD,
                        half * 128 : half * 128 + 128,
                    ] = rows.astype(jnp.bfloat16)


def whiten(samples, live):
    return pl.pallas_call(
        whiten_kernel,
        grid=(SEG_DEV // STEP,),
        out_shape=(
            jax.ShapeDtypeStruct((N_SEG, BAND, 2 * SEG_PAD, CH), jnp.bfloat16),
            jax.ShapeDtypeStruct((1, 128), jnp.float32),
        ),
        in_specs=[
            pl.BlockSpec((STEP, CH, L), lambda i: (i, 0, 0)),
            pl.BlockSpec((L, 2 * F), lambda i: (0, 0)),
            pl.BlockSpec((1, CH), lambda i: (0, 0)),
            pl.BlockSpec((CH, 1), lambda i: (0, 0)),
            pl.BlockSpec((F, CH), lambda i: (0, 0)),
        ],
        out_specs=(
            pl.BlockSpec((N_SEG, BAND, 2 * SEG_PAD, CH), lambda i: (0, 0, 0, 0)),
            pl.BlockSpec((1, 128), lambda i: (0, 0)),
        ),
        scratch_shapes=[
            pltpu.VMEM((2, SEG_PAD * 2 * F, 128), jnp.float32),
            pltpu.VMEM((F + 16, CH), jnp.float32),
        ],
        compiler_params=pltpu.CompilerParams(vmem_limit_bytes=32 << 20),
    )(
        samples,
        jnp.asarray(dft_table()),
        live.reshape(1, CH),
        live.reshape(CH, 1),
        jnp.asarray(inverse_counts()),
    )


def exchange_kernel(
    white_ref,
    power_ref,
    bands_ref,
    weights_ref,
    parts,
    own_weights,
    power_send,
    power_recv,
    weight_send,
    weight_recv,
    seg_send,
    seg_recv,
    local_sem,
    own_y_send,
    own_x_send,
    fwd_x_send,
    core_a_send,
    core_b_send,
    slot_recv,
):
    chan = lax.axis_index("chan")
    seg = lax.axis_index("seg")
    y = chan // 4
    x_hi = (chan // 2) % 2
    core = chan % 2

    barrier = pltpu.get_barrier_semaphore()

    def greet(i, carry):
        pl.semaphore_signal(
            barrier, inc=1, device_id=(chan, (seg + i) % N_SEG), device_id_type=MESH
        )
        pl.semaphore_signal(
            barrier, inc=1, device_id=((chan + i) % N_CHAN, seg), device_id_type=MESH
        )
        return carry

    lax.fori_loop(1, 16, greet, 0)
    pl.semaphore_wait(barrier, 30)

    def power_copy(i):
        return pltpu.make_async_remote_copy(
            src_ref=power_ref,
            dst_ref=parts.at[chan],
            send_sem=power_send.at[i],
            recv_sem=power_recv.at[i],
            device_id=((chan + i) % N_CHAN, seg),
            device_id_type=MESH,
        )

    def seg_copy(f, i):
        target = (seg + i) % N_SEG
        return pltpu.make_async_remote_copy(
            src_ref=white_ref.at[target, f],
            dst_ref=bands_ref.at[0, f, seg],
            send_sem=seg_send.at[f, i],
            recv_sem=seg_recv.at[f, i],
            device_id=(chan, target),
            device_id_type=MESH,
        )

    def local_copy(f):
        return pltpu.make_async_copy(
            white_ref.at[seg, f], bands_ref.at[0, f, seg], local_sem.at[f]
        )

    def weight_copy(i):
        return pltpu.make_async_remote_copy(
            src_ref=own_weights,
            dst_ref=weights_ref.at[seg],
            send_sem=weight_send.at[i],
            recv_sem=weight_recv.at[i],
            device_id=(chan, (seg + i) % N_SEG),
            device_id_type=MESH,
        )

    def block_copy(source, slot, f, send, target):
        return pltpu.make_async_remote_copy(
            src_ref=bands_ref.at[source, f],
            dst_ref=bands_ref.at[slot, f],
            send_sem=send.at[f],
            recv_sem=slot_recv.at[slot, f],
            device_id=(target, seg),
            device_id_type=MESH,
        )

    def each(first, last, fn):
        def body(i, carry):
            fn(i)
            return carry

        lax.fori_loop(first, last, body, 0)

    each(1, 16, lambda i: power_copy(i).start())
    for f in range(BAND):
        each(1, 16, lambda i: seg_copy(f, i).start())
        local_copy(f).start()

    parts[chan] = power_ref[...]
    each(1, 16, lambda i: power_copy(i).wait())
    total = jnp.sum(parts[...], axis=0)
    lane = lax.broadcasted_iota(jnp.int32, (1, 128), 1)
    weights = 1.0 / jnp.sqrt(total / (CHANNELS * L) + eps_power)
    weights = jnp.where(lane < SEG_DEV, weights, 0.0)
    own_weights[...] = weights
    weights_ref[seg] = weights
    each(1, 16, lambda i: weight_copy(i).start())

    other = chan + 1 - 2 * core
    own_y = functools.partial(block_copy, 0, 4, send=own_y_send, target=(chan + 12) % 16)
    own_x = functools.partial(block_copy, 0, 2, send=own_x_send, target=chan // 4 * 4 + core)
    fwd_x = functools.partial(block_copy, 4, 2, send=fwd_x_send, target=chan // 4 * 4 + 2 + core)
    even_a = functools.partial(block_copy, 2, 1, send=core_a_send, target=other)
    even_b = functools.partial(block_copy, 4, 3, send=core_b_send, target=other)
    odd_a = functools.partial(block_copy, 0, 1, send=core_a_send, target=other)
    odd_b = functools.partial(block_copy, 2, 3, send=core_b_send, target=other)

    has_near = jnp.logical_or(y < 3, x_hi == 0)
    has_far = y < 3

    def arrived(slot, f):
        block_copy(0, slot, f, own_y_send, chan).wait_recv()

    def send_own(f):
        @pl.when(y > 0)
        def _():
            own_y(f=f).start()

        @pl.when(x_hi == 1)
        def _():
            own_x(f=f).start()

        @pl.when(core == 1)
        def _():
            odd_a(f=f).start()

    def forward_far(f):
        @pl.when(has_far)
        def _():
            arrived(4, f)

            @pl.when(x_hi == 0)
            def _():
                fwd_x(f=f).start()

            @pl.when(core == 0)
            def _():
                even_b(f=f).start()

    def forward_near(f):
        @pl.when(has_near)
        def _():
            arrived(2, f)

            @pl.when(core == 0)
            def _():
                even_a(f=f).start()

            @pl.when(core == 1)
            def _():
                odd_b(f=f).start()

    for f in range(BAND):
        local_copy(f).wait()
        each(1, 16, lambda i: seg_copy(f, i).wait_recv())
        send_own(f)
        if f > 0:
            forward_far(f - 1)
        if f > 1:
            forward_near(f - 2)
    forward_far(BAND - 1)
    forward_near(BAND - 2)
    forward_near(BAND - 1)

    for f in range(BAND):

        @pl.when(jnp.logical_or(core == 0, has_near))
        def _():
            arrived(1, f)

        @pl.when(jnp.logical_or(jnp.logical_and(core == 0, has_near), has_far))
        def _():
            arrived(3, f)

        each(1, 16, lambda i: seg_copy(f, i).wait_send())

        @pl.when(y > 0)
        def _():
            own_y(f=f).wait_send()

        @pl.when(x_hi == 1)
        def _():
            own_x(f=f).wait_send()

        @pl.when(jnp.logical_and(has_far, x_hi == 0))
        def _():
            fwd_x(f=f).wait_send()

        @pl.when(jnp.logical_or(core == 1, has_near))
        def _():
            even_a(f=f).wait_send()

        @pl.when(jnp.logical_or(jnp.logical_and(core == 1, has_near), jnp.logical_and(core == 0, has_far)))
        def _():
            even_b(f=f).wait_send()

    each(1, 16, lambda i: weight_copy(i).wait())


def exchange(white, power):
    dma = pltpu.SemaphoreType.DMA
    return pl.pallas_call(
        exchange_kernel,
        out_shape=(
            jax.ShapeDtypeStruct((NEAR, BAND, N_SEG, 2 * SEG_PAD, CH), jnp.bfloat16),
            jax.ShapeDtypeStruct((N_SEG, 1, 128), jnp.float32),
        ),
        in_specs=[pl.BlockSpec(memory_space=pltpu.VMEM)] * 2,
        out_specs=(
            pl.BlockSpec(memory_space=pl.ANY),
            pl.BlockSpec(memory_space=pltpu.VMEM),
        ),
        scratch_shapes=[
            pltpu.VMEM((N_CHAN, 1, 128), jnp.float32),
            pltpu.VMEM((1, 128), jnp.float32),
            dma((16,)),
            dma((16,)),
            dma((16,)),
            dma((16,)),
            dma((BAND, 16)),
            dma((BAND, 16)),
            dma((BAND,)),
            dma((BAND,)),
            dma((BAND,)),
            dma((BAND,)),
            dma((BAND,)),
            dma((BAND,)),
            dma((NEAR, BAND)),
        ],
        compiler_params=pltpu.CompilerParams(
            collective_id=0, has_side_effects=True, vmem_limit_bytes=32 << 20
        ),
    )(white, power)


def cross_kernel(chan_ref, bands_ref, weights_ref, out_ref, left):
    lane = lax.broadcasted_iota(jnp.int32, (SEG_PAD, 128), 1)
    row = lax.broadcasted_iota(jnp.int32, (SEG_PAD, 128), 0)
    factor = math.sqrt(SEGMENTS) / jnp.sum(weights_ref[...])
    for source in range(N_SEG):
        spread = jnp.broadcast_to(weights_ref[source], (SEG_PAD, 128))
        scale = jnp.sum(jnp.where(lane == row, spread, 0.0), axis=1, keepdims=True) * factor
        real = bands_ref[0, 0, source, :SEG_PAD, :].astype(jnp.float32) * scale
        imag = bands_ref[0, 0, source, SEG_PAD:, :].astype(jnp.float32) * scale
        first = source * 2 * SEG_PAD
        left[0, first : first + SEG_PAD, :] = real.astype(jnp.bfloat16)
        left[0, first + SEG_PAD : first + 2 * SEG_PAD, :] = imag.astype(jnp.bfloat16)
        left[1, first : first + SEG_PAD, :] = (-imag).astype(jnp.bfloat16)
        left[1, first + SEG_PAD : first + 2 * SEG_PAD, :] = real.astype(jnp.bfloat16)
    block = chan_ref[0]
    mine = lax.broadcasted_iota(jnp.int32, (CH, CH), 0)
    theirs = lax.broadcasted_iota(jnp.int32, (CH, CH), 1)
    for r in range(2):
        rows = left[r].T
        for k in range(NEAR):
            partner = bands_ref[k, 0].reshape(N_SEG * 2 * SEG_PAD, CH)
            product = jnp.dot(rows, partner, preferred_element_type=jnp.float32)
            keep = block + k < N_CHAN
            if k == 0:
                keep = jnp.logical_and(keep, theirs > mine)
            if k == REACH:
                keep = jnp.logical_and(keep, theirs <= mine)
            product = jnp.where(keep, product, 0.0)
            out_ref[0, k, :, r * CH : (r + 1) * CH] = product.astype(jnp.bfloat16)


def cross(chan, bands, weights):
    return pl.pallas_call(
        cross_kernel,
        grid=(BAND,),
        out_shape=jax.ShapeDtypeStruct((BAND, NEAR, CH, 2 * CH), jnp.bfloat16),
        in_specs=[
            pl.BlockSpec(memory_space=pltpu.SMEM),
            pl.BlockSpec((NEAR, 1, N_SEG, 2 * SEG_PAD, CH), lambda f: (0, f, 0, 0, 0)),
            pl.BlockSpec((N_SEG, 1, 128), lambda f: (0, 0, 0)),
        ],
        out_specs=pl.BlockSpec((1, NEAR, CH, 2 * CH), lambda f: (f, 0, 0, 0)),
        scratch_shapes=[pltpu.VMEM((2, N_SEG * 2 * SEG_PAD, CH), jnp.bfloat16)],
        compiler_params=pltpu.CompilerParams(vmem_limit_bytes=32 << 20),
    )(chan, bands, weights)


def on_device(samples, live_trace):
    by_segment = jnp.transpose(samples, (1, 0, 2))
    live = live_trace.astype(jnp.float32)
    white, power = whiten(by_segment, live)
    bands, weights = exchange(white, power)
    chan = lax.axis_index("chan").reshape(1)
    stacked = cross(chan, bands, weights)
    return jnp.transpose(stacked, (0, 2, 1, 3))


def solution(mesh):
    in_specs = (P("chan", "seg", None), P("chan"))
    out_specs = P("seg", "chan", None, None)
    return jax.shard_map(
        on_device, mesh=mesh, in_specs=in_specs, out_specs=out_specs, check_vma=False
    )
```

```python
import functools
import math

import jax
import jax.numpy as jnp
import numpy as np
from jax import lax
from jax.experimental import pallas as pl
from jax.experimental.pallas import tpu as pltpu
from jax.sharding import PartitionSpec as P

L = 1024
F = 64
F0 = 16
REACH = 4
NEAR = 5
CH = 256
CHANNELS = 4096
SEGMENTS = 240
N_CHAN = 16
N_SEG = 16
SEG_DEV = 15
SEG_PAD = 16
HALF = 8
BAND = F // N_SEG
VMEM_LIMIT = 40 << 20
CHUNKS = ((0, 0, 2), (0, 2, 2), (1, 0, 2), (1, 2, 1), (1, 3, 1))

eps_power = 1e-06
water_level = 0.1
smooth_half = 2

MESH = pl.DeviceIdType.MESH


def dft_table():
    time_index = np.arange(L)
    bin_number = np.arange(F) + F0
    phase_step = (time_index[:, None] * bin_number[None, :] % L).astype(np.float32)
    angle = phase_step * np.float32(2.0 * math.pi / L)
    taper = np.float32(0.5) - np.float32(0.5) * np.cos(
        time_index.astype(np.float32) * np.float32(2.0 * math.pi / L)
    )
    real = taper[:, None] * np.cos(angle)
    imag = -taper[:, None] * np.sin(angle)
    return np.concatenate([real, imag], axis=1).astype(jnp.bfloat16)


def each(first, last, fn):
    def step(i, carry):
        fn(i)
        return carry

    lax.fori_loop(first, last, step, 0)


def exchange_kernel(
    samples_ref,
    table_hbm,
    live_hbm,
    bands_ref,
    weights_ref,
    live_ref,
    samples,
    table,
    live_column,
    inverse,
    padded,
    energy,
    wide,
    white,
    aside,
    power,
    parts,
    own_weights,
    load_sem,
    table_sem,
    live_sem,
    power_send,
    power_recv,
    weight_send,
    weight_recv,
    z_send,
    z_recv,
    local_sem,
    pass_send,
    pass_recv,
    y_send,
    x_send,
    cross_send,
    core_a_send,
    core_b_send,
    slot_recv,
):
    chan = lax.axis_index("chan")
    seg = lax.axis_index("seg")
    y = chan // 4
    x_hi = (chan // 2) % 2
    core = chan % 2
    x_lo = seg // 8
    z = seg % 8

    def load(j):
        return pltpu.make_async_copy(samples_ref.at[j], samples.at[j], load_sem.at[j])

    load_table = pltpu.make_async_copy(table_hbm, table, table_sem)
    load_live = pltpu.make_async_copy(live_hbm, live_ref, live_sem)
    load_live.start()
    load_table.start()
    each(0, SEG_DEV, lambda j: load(j).start())

    barrier = pltpu.get_barrier_semaphore()

    def greet(i):
        pl.semaphore_signal(
            barrier, inc=1, device_id=(chan, (seg + i) % N_SEG), device_id_type=MESH
        )
        pl.semaphore_signal(
            barrier, inc=1, device_id=((chan + i) % N_CHAN, seg), device_id_type=MESH
        )

    each(1, 16, greet)
    pl.semaphore_signal(
        barrier,
        inc=1,
        device_id=(chan + 2 - 4 * x_hi, (1 - x_lo) * 8 + z),
        device_id_type=MESH,
    )

    load_live.wait()
    live_row = live_ref[...].astype(jnp.float32)
    live_column[...] = jnp.broadcast_to(live_row, (128, CH)).T
    bins = lax.broadcasted_iota(jnp.int32, (F, CH), 0)
    count = jnp.minimum(bins, smooth_half) + jnp.minimum(F - 1 - bins, smooth_half) + 1
    inverse[...] = 1.0 / count.astype(jnp.float32)
    padded[...] = jnp.zeros_like(padded)
    energy[...] = jnp.zeros_like(energy)
    for half in range(2):
        wide[1, half, (HALF - 1) * 2 * F :, :] = jnp.zeros((2 * F, 128), jnp.float32)
    load_table.wait()

    def whiten(j, slot):
        x = samples[j]
        spectra = jnp.dot(x, table[...], preferred_element_type=jnp.float32)
        squares = jnp.zeros((CH, 128), jnp.float32)
        for tile in range(L // 128):
            part = x[:, tile * 128 : (tile + 1) * 128].astype(jnp.float32)
            squares += part * part
        energy[j] = jnp.sum(squares * live_column[...], axis=0, keepdims=True)
        spectra = spectra.T
        real = spectra[:F]
        imag = spectra[F:]
        level = real * real + imag * imag
        padded[slot, 8 : 8 + F, :] = level
        near = level
        for distance in (-2, -1, 1, 2):
            near += padded[slot, 8 + distance : 8 + distance + F, :]
        mean = jnp.sum(level, axis=0, keepdims=True) * (water_level / F)
        gain = live_row / jnp.sqrt(near * inverse[...] + mean + eps_power)
        real = real * gain
        imag = imag * gain
        base = pl.multiple_of((j % HALF) * 2 * F, 2 * F)
        for half in range(2):
            lanes = slice(half * 128, half * 128 + 128)
            wide[j // HALF, half, pl.ds(base, F), :] = real[:, lanes]
            wide[j // HALF, half, pl.ds(base + F, F), :] = imag[:, lanes]

    def whiten_pair(i):
        load(2 * i).wait()
        load(2 * i + 1).wait()
        whiten(2 * i, 0)
        whiten(2 * i + 1, 1)

    def arrange(sh, f0, nf):
        for f in range(f0, f0 + nf):
            for band in range(N_SEG):
                for half in range(2):
                    rows = [
                        wide[sh, half, pl.ds(r * F + band * BAND + f, HALF, stride=2 * F), :]
                        for r in range(2)
                    ]
                    white[sh, band, f, :, half * 128 : half * 128 + 128] = jnp.concatenate(
                        rows, axis=0
                    ).astype(jnp.bfloat16)

    def z_copy(t, i):
        sh, f0, nf = CHUNKS[t]
        target = (z + i) % 8
        keep = pltpu.make_async_remote_copy(
            src_ref=white.at[sh, x_lo * 8 + target, pl.ds(f0, nf)],
            dst_ref=bands_ref.at[0, sh, pl.ds(f0, nf), x_lo * 8 + z],
            send_sem=z_send.at[t, 0, i],
            recv_sem=z_recv.at[t, 0, i],
            device_id=(chan, x_lo * 8 + target),
            device_id_type=MESH,
        )
        hand = pltpu.make_async_remote_copy(
            src_ref=white.at[sh, (1 - x_lo) * 8 + target, pl.ds(f0, nf)],
            dst_ref=aside.at[sh, pl.ds(f0, nf), z],
            send_sem=z_send.at[t, 1, i],
            recv_sem=z_recv.at[t, 1, i],
            device_id=(chan, x_lo * 8 + target),
            device_id_type=MESH,
        )
        return keep, hand

    def local_copy(t):
        sh, f0, nf = CHUNKS[t]
        keep = pltpu.make_async_copy(
            white.at[sh, x_lo * 8 + z, pl.ds(f0, nf)],
            bands_ref.at[0, sh, pl.ds(f0, nf), x_lo * 8 + z],
            local_sem.at[t, 0],
        )
        hand = pltpu.make_async_copy(
            white.at[sh, (1 - x_lo) * 8 + z, pl.ds(f0, nf)],
            aside.at[sh, pl.ds(f0, nf), z],
            local_sem.at[t, 1],
        )
        return keep, hand

    def send_chunk(t):
        def one(i):
            for copy in z_copy(t, i):
                copy.start()

        each(1, 8, one)
        for copy in local_copy(t):
            copy.start()

    def part_of(slot, t, side):
        sh, f0, nf = CHUNKS[t]
        return bands_ref.at[slot, sh, pl.ds(f0, nf), pl.ds(side * 8, 8)]

    def block_copy(source, slot, send, target, t, side, part):
        return pltpu.make_async_remote_copy(
            src_ref=part_of(source, t, side),
            dst_ref=part_of(slot, t, side),
            send_sem=send.at[t, part],
            recv_sem=slot_recv.at[slot, t, part],
            device_id=(target, seg),
            device_id_type=MESH,
        )

    def aside_copy(t, slot, send, recv, target):
        sh, f0, nf = CHUNKS[t]
        return pltpu.make_async_remote_copy(
            src_ref=aside.at[sh, pl.ds(f0, nf)],
            dst_ref=part_of(slot, t, x_lo),
            send_sem=send,
            recv_sem=recv,
            device_id=(target, (1 - x_lo) * 8 + z),
            device_id_type=MESH,
        )

    def side_of(part):
        return x_lo if part == 0 else 1 - x_lo

    def pass_copy(t):
        return aside_copy(t, 0, pass_send.at[t], pass_recv.at[t], chan)

    def cross_own(t):
        return block_copy(0, 2, cross_send, chan // 4 * 4 + core, t, x_lo, 0)

    def cross_other(t):
        return aside_copy(
            t, 2, cross_send.at[t, 1], slot_recv.at[2, t, 1], chan // 4 * 4 + core
        )

    def down_copy(t, part):
        return block_copy(0, 4, y_send, (chan + 12) % 16, t, side_of(part), part)

    def forward_copy(t, part):
        return block_copy(4, 2, x_send, chan // 4 * 4 + 2 + core, t, side_of(part), part)

    other = chan + 1 - 2 * core

    def core_copy(source, slot, t, part):
        send = core_a_send if slot == 1 else core_b_send
        return block_copy(source, slot, send, other, t, side_of(part), part)

    def arrived(slot, t, part):
        block_copy(0, slot, y_send, other, t, side_of(part), part).wait_recv()

    has_near = jnp.logical_or(y < 3, x_hi == 0)
    has_far = y < 3

    def send_own(t, part):
        @pl.when(y > 0)
        def _():
            down_copy(t, part).start()

        @pl.when(core == 1)
        def _():
            core_copy(0, 1, t, part).start()

    def after_z(t):
        def one(i):
            for copy in z_copy(t, i):
                copy.wait_recv()

        each(1, 8, one)
        for copy in local_copy(t):
            copy.wait()
        pass_copy(t).start()
        send_own(t, 0)

        @pl.when(x_hi == 1)
        def _():
            cross_other(t).start()
            cross_own(t).start()

    def after_pass(t):
        pass_copy(t).wait_recv()
        send_own(t, 1)

    def after_far(t):
        @pl.when(has_far)
        def _():
            for part in range(2):
                arrived(4, t, part)

                @pl.when(x_hi == 0)
                def _():
                    forward_copy(t, part).start()

                @pl.when(core == 0)
                def _():
                    core_copy(4, 3, t, part).start()

    def after_near(t):
        @pl.when(has_near)
        def _():
            for part in range(2):
                arrived(2, t, part)

                @pl.when(core == 0)
                def _():
                    core_copy(2, 1, t, part).start()

                @pl.when(core == 1)
                def _():
                    core_copy(2, 3, t, part).start()

    def power_copy(i):
        return pltpu.make_async_remote_copy(
            src_ref=power,
            dst_ref=parts.at[chan],
            send_sem=power_send.at[i],
            recv_sem=power_recv.at[i],
            device_id=((chan + i) % N_CHAN, seg),
            device_id_type=MESH,
        )

    def weight_copy(i):
        return pltpu.make_async_remote_copy(
            src_ref=own_weights,
            dst_ref=weights_ref.at[seg],
            send_sem=weight_send.at[i],
            recv_sem=weight_recv.at[i],
            device_id=(chan, (seg + i) % N_SEG),
            device_id_type=MESH,
        )

    each(0, HALF // 2, whiten_pair)
    first = True
    for t, chunk in enumerate(CHUNKS):
        if chunk[0] == 0:
            arrange(*chunk)
            if first:
                pl.semaphore_wait(barrier, 31)
                first = False
            send_chunk(t)
    each(HALF // 2, HALF - 1, whiten_pair)
    load(SEG_DEV - 1).wait()
    whiten(SEG_DEV - 1, 0)
    for t, chunk in enumerate(CHUNKS):
        if chunk[0] == 1:
            arrange(*chunk)
            send_chunk(t)

    lane = lax.broadcasted_iota(jnp.int32, (SEG_PAD, 1, 128), 2)
    row = lax.broadcasted_iota(jnp.int32, (SEG_PAD, 1, 128), 0)
    totals = jnp.sum(energy[...], axis=2, keepdims=True)
    power[...] = jnp.sum(jnp.where(lane == row, totals, 0.0), axis=0)
    each(1, 16, lambda i: power_copy(i).start())
    parts[chan] = power[...]
    each(1, 16, lambda i: power_copy(i).wait())
    total = jnp.sum(parts[...], axis=0)
    lane = lax.broadcasted_iota(jnp.int32, (1, 128), 1)
    weights = 1.0 / jnp.sqrt(total / (CHANNELS * L) + eps_power)
    weights = jnp.where(lane < SEG_DEV, weights, 0.0)
    own_weights[...] = weights
    weights_ref[seg] = weights
    each(1, 16, lambda i: weight_copy(i).start())

    n = len(CHUNKS)
    for step in range(n + 3):
        if step < n:
            after_z(step)
        if 0 <= step - 1 < n:
            after_pass(step - 1)
        if 0 <= step - 2 < n:
            after_far(step - 2)
        if 0 <= step - 3 < n:
            after_near(step - 3)

    for t in range(n):
        for part in range(2):

            @pl.when(jnp.logical_or(core == 0, has_near))
            def _():
                arrived(1, t, part)

            @pl.when(jnp.logical_or(jnp.logical_and(core == 0, has_near), has_far))
            def _():
                arrived(3, t, part)

    for t in range(n):

        def done(i):
            for copy in z_copy(t, i):
                copy.wait_send()

        each(1, 8, done)
        pass_copy(t).wait_send()

        @pl.when(x_hi == 1)
        def _():
            cross_other(t).wait_send()
            cross_own(t).wait_send()

        for part in range(2):

            @pl.when(y > 0)
            def _():
                down_copy(t, part).wait_send()

            @pl.when(jnp.logical_and(has_far, x_hi == 0))
            def _():
                forward_copy(t, part).wait_send()

            @pl.when(jnp.logical_or(core == 1, has_near))
            def _():
                core_copy(0, 1, t, part).wait_send()

            @pl.when(
                jnp.logical_or(
                    jnp.logical_and(core == 1, has_near), jnp.logical_and(core == 0, has_far)
                )
            )
            def _():
                core_copy(0, 3, t, part).wait_send()

    each(1, 16, lambda i: weight_copy(i).wait())


def exchange(samples, live):
    dma = pltpu.SemaphoreType.DMA
    n = len(CHUNKS)
    return pl.pallas_call(
        exchange_kernel,
        out_shape=(
            jax.ShapeDtypeStruct((NEAR, 2, BAND, N_SEG, 2 * HALF, CH), jnp.bfloat16),
            jax.ShapeDtypeStruct((N_SEG, 1, 128), jnp.float32),
        ),
        in_specs=[
            pl.BlockSpec(memory_space=pltpu.HBM),
            pl.BlockSpec(memory_space=pltpu.HBM),
            pl.BlockSpec(memory_space=pltpu.HBM),
        ],
        out_specs=(
            pl.BlockSpec(memory_space=pltpu.VMEM),
            pl.BlockSpec(memory_space=pltpu.VMEM),
        ),
        scratch_shapes=[
            pltpu.VMEM((1, CH), jnp.int32),
            pltpu.VMEM((SEG_DEV, CH, L), jnp.bfloat16),
            pltpu.VMEM((L, 2 * F), jnp.bfloat16),
            pltpu.VMEM((CH, 128), jnp.float32),
            pltpu.VMEM((F, CH), jnp.float32),
            pltpu.VMEM((2, F + 16, CH), jnp.float32),
            pltpu.VMEM((SEG_PAD, 1, 128), jnp.float32),
            pltpu.VMEM((2, 2, HALF * 2 * F, 128), jnp.float32),
            pltpu.VMEM((2, N_SEG, BAND, 2 * HALF, CH), jnp.bfloat16),
            pltpu.VMEM((2, BAND, 8, 2 * HALF, CH), jnp.bfloat16),
            pltpu.VMEM((1, 128), jnp.float32),
            pltpu.VMEM((N_CHAN, 1, 128), jnp.float32),
            pltpu.VMEM((1, 128), jnp.float32),
            dma((SEG_DEV,)),
            dma,
            dma,
            dma((16,)),
            dma((16,)),
            dma((16,)),
            dma((16,)),
            dma((n, 2, 8)),
            dma((n, 2, 8)),
            dma((n, 2)),
            dma((n,)),
            dma((n,)),
            dma((n, 2)),
            dma((n, 2)),
            dma((n, 2)),
            dma((n, 2)),
            dma((n, 2)),
            dma((NEAR, n, 2)),
        ],
        compiler_params=pltpu.CompilerParams(
            collective_id=0, has_side_effects=True, vmem_limit_bytes=VMEM_LIMIT
        ),
    )(*[
        pltpu.with_memory_space_constraint(value, pltpu.HBM)
        for value in (samples, jnp.asarray(dft_table()), live)
    ])


def cross_kernel(chan_ref, bands_ref, weights_ref, out_ref, left, result, out_sem):
    lane = lax.broadcasted_iota(jnp.int32, (HALF, 128), 1)
    row = lax.broadcasted_iota(jnp.int32, (HALF, 128), 0)
    factor = math.sqrt(SEGMENTS) / jnp.sum(weights_ref[...])
    block = chan_ref[0]
    mine = lax.broadcasted_iota(jnp.int32, (CH, CH), 0)
    theirs = lax.broadcasted_iota(jnp.int32, (CH, CH), 1)
    for f in range(BAND):
        for sh in range(2):
            for source in range(N_SEG):
                spread = jnp.broadcast_to(weights_ref[source], (HALF, 128))
                scale = jnp.where(lane == row + sh * HALF, spread, 0.0)
                scale = jnp.sum(scale, axis=1, keepdims=True) * factor
                both = bands_ref[0, sh, f, source].astype(jnp.float32)
                real = both[:HALF] * scale
                imag = both[HALF:] * scale
                first = (sh * N_SEG + source) * 2 * HALF
                rows = slice(first, first + 2 * HALF)
                left[f % 2, 0, rows, :] = jnp.concatenate([real, imag], axis=0).astype(jnp.bfloat16)
                left[f % 2, 1, rows, :] = jnp.concatenate([-imag, real], axis=0).astype(jnp.bfloat16)
        turned = [left[f % 2, r].T for r in range(2)]
        for k in range(NEAR):
            for r in range(2):
                product = jnp.zeros((CH, CH), jnp.float32)
                for sh in range(2):
                    partner = bands_ref[k, sh, f].reshape(CH, CH)
                    product += jnp.dot(
                        turned[r][:, sh * CH : (sh + 1) * CH],
                        partner,
                        preferred_element_type=jnp.float32,
                    )
                keep = block + k < N_CHAN
                if k == 0:
                    keep = jnp.logical_and(keep, theirs > mine)
                if k == REACH:
                    keep = jnp.logical_and(keep, theirs <= mine)
                product = jnp.where(keep, product, 0.0)
                result[f, k, :, r * CH : (r + 1) * CH] = product.astype(jnp.bfloat16)
            pltpu.make_async_copy(result.at[f, k], out_ref.at[f, k], out_sem.at[f, k]).start()
    for f in range(BAND):
        for k in range(NEAR):
            pltpu.make_async_copy(result.at[f, k], out_ref.at[f, k], out_sem.at[f, k]).wait()


def cross(chan, bands, weights):
    return pl.pallas_call(
        cross_kernel,
        out_shape=jax.ShapeDtypeStruct((BAND, NEAR, CH, 2 * CH), jnp.bfloat16),
        in_specs=[
            pl.BlockSpec(memory_space=pltpu.SMEM),
            pl.BlockSpec(memory_space=pltpu.VMEM),
            pl.BlockSpec(memory_space=pltpu.VMEM),
        ],
        out_specs=pl.BlockSpec(memory_space=pltpu.HBM),
        scratch_shapes=[
            pltpu.VMEM((2, 2, N_SEG * 2 * SEG_PAD, CH), jnp.bfloat16),
            pltpu.VMEM((BAND, NEAR, CH, 2 * CH), jnp.bfloat16),
            pltpu.SemaphoreType.DMA((BAND, NEAR)),
        ],
        compiler_params=pltpu.CompilerParams(vmem_limit_bytes=40 << 20),
    )(chan, bands, weights)


def on_device(samples, live_trace):
    by_segment = jnp.transpose(samples, (1, 0, 2))
    bands, weights = exchange(by_segment, live_trace.reshape(1, CH))
    chan = lax.axis_index("chan").reshape(1)
    stacked = cross(chan, bands, weights)
    return jnp.transpose(stacked, (0, 2, 1, 3))


def solution(mesh):
    in_specs = (P("chan", "seg", None), P("chan"))
    out_specs = P("seg", "chan", None, None)
    return jax.shard_map(
        on_device, mesh=mesh, in_specs=in_specs, out_specs=out_specs, check_vma=False
    )
```

```python
import functools
import math

import jax
import jax.numpy as jnp
import numpy as np
from jax import lax
from jax.experimental import pallas as pl
from jax.experimental.pallas import tpu as pltpu
from jax.sharding import PartitionSpec as P

L = 1024
F = 64
F0 = 16
REACH = 4
NEAR = 5
CH = 256
CHANNELS = 4096
SEGMENTS = 240
N_CHAN = 16
N_SEG = 16
SEG_DEV = 15
SEG_PAD = 16
HALF = 8
BAND = F // N_SEG
GROUP = 4
DIRECT = (1, 3, 5, 6, 7)
VMEM_LIMIT = 40 << 20
CHUNKS = tuple((t // 4, t % 4, 1) for t in range(8))

eps_power = 1e-06
water_level = 0.1
smooth_half = 2

MESH = pl.DeviceIdType.MESH


def dft_table():
    time_index = np.arange(L)
    bin_number = np.arange(F) + F0
    phase_step = (time_index[:, None] * bin_number[None, :] % L).astype(np.float32)
    angle = phase_step * np.float32(2.0 * math.pi / L)
    taper = np.float32(0.5) - np.float32(0.5) * np.cos(
        time_index.astype(np.float32) * np.float32(2.0 * math.pi / L)
    )
    real = taper[:, None] * np.cos(angle)
    imag = -taper[:, None] * np.sin(angle)
    return np.concatenate([real, imag], axis=1).astype(jnp.bfloat16)


def each(first, last, fn):
    def step(i, carry):
        fn(i)
        return carry

    lax.fori_loop(first, last, step, 0)


def exchange_kernel(
    samples_ref,
    table_hbm,
    live_hbm,
    bands_ref,
    weights_ref,
    live_ref,
    samples,
    table,
    live_column,
    inverse,
    padded,
    energy,
    wide,
    white,
    aside,
    far_aside,
    power,
    parts,
    own_weights,
    load_sem,
    table_sem,
    live_sem,
    power_send,
    power_recv,
    weight_send,
    weight_recv,
    z_send,
    z_recv,
    pass_send,
    pass_recv,
    y_send,
    x_send,
    cross_send,
    core_a_send,
    core_b_send,
    slot_recv,
    aside_send,
    aside_recv,
):
    chan = lax.axis_index("chan")
    seg = lax.axis_index("seg")
    y = chan // 4
    x_hi = (chan // 2) % 2
    core = chan % 2
    x_lo = seg // 8
    z = seg % 8

    def load(j):
        return pltpu.make_async_copy(samples_ref.at[j], samples.at[j], load_sem.at[j])

    load_table = pltpu.make_async_copy(table_hbm, table, table_sem)
    load_live = pltpu.make_async_copy(live_hbm, live_ref, live_sem)
    load_live.start()
    load_table.start()
    each(0, SEG_DEV, lambda j: load(j).start())

    barrier = pltpu.get_barrier_semaphore()

    def greet(i):
        pl.semaphore_signal(
            barrier, inc=1, device_id=(chan, (seg + i) % N_SEG), device_id_type=MESH
        )
        pl.semaphore_signal(
            barrier, inc=1, device_id=((chan + i) % N_CHAN, seg), device_id_type=MESH
        )

    each(1, 16, greet)
    pl.semaphore_signal(
        barrier,
        inc=1,
        device_id=(chan + 2 - 4 * x_hi, (1 - x_lo) * 8 + z),
        device_id_type=MESH,
    )

    load_live.wait()
    live_row = live_ref[...].astype(jnp.float32)
    live_column[...] = jnp.broadcast_to(live_row, (128, CH)).T
    bins = lax.broadcasted_iota(jnp.int32, (F, CH), 0)
    count = jnp.minimum(bins, smooth_half) + jnp.minimum(F - 1 - bins, smooth_half) + 1
    inverse[...] = 1.0 / count.astype(jnp.float32)
    padded[...] = jnp.zeros_like(padded)
    samples[SEG_DEV] = jnp.zeros((CH, L), jnp.bfloat16)
    load_table.wait()

    def whiten(j, slot):
        x = samples[j]
        spectra = jnp.dot(x, table[...], preferred_element_type=jnp.float32)
        squares = jnp.zeros((CH, 128), jnp.float32)
        for tile in range(L // 128):
            part = x[:, tile * 128 : (tile + 1) * 128].astype(jnp.float32)
            squares += part * part
        energy[j] = jnp.sum(squares * live_column[...], axis=0, keepdims=True)
        spectra = spectra.T
        real = spectra[:F]
        imag = spectra[F:]
        level = real * real + imag * imag
        padded[slot, 8 : 8 + F, :] = level
        near = level
        for distance in (-2, -1, 1, 2):
            near += padded[slot, 8 + distance : 8 + distance + F, :]
        mean = jnp.sum(level, axis=0, keepdims=True) * (water_level / F)
        gain = live_row / jnp.sqrt(near * inverse[...] + mean + eps_power)
        real = real * gain
        imag = imag * gain
        base = pl.multiple_of((j % HALF) * 2 * F, 2 * F)
        for half in range(2):
            lanes = slice(half * 128, half * 128 + 128)
            wide[j // HALF, half, pl.ds(base, F), :] = real[:, lanes]
            wide[j // HALF, half, pl.ds(base + F, F), :] = imag[:, lanes]

    def whiten_group(i):
        for slot in range(GROUP - 1):
            load(GROUP * i + slot).wait()

        @pl.when(GROUP * i + GROUP - 1 < SEG_DEV)
        def _():
            load(GROUP * i + GROUP - 1).wait()

        for slot in range(GROUP):
            whiten(GROUP * i + slot, slot)

    def arrange(sh, f0, nf):
        for f in range(f0, f0 + nf):
            for band in range(N_SEG):
                for half in range(2):
                    rows = [
                        wide[sh, half, pl.ds(r * F + band * BAND + f, HALF, stride=2 * F), :]
                        for r in range(2)
                    ]
                    white[sh, band, f, :, half * 128 : half * 128 + 128] = jnp.concatenate(
                        rows, axis=0
                    ).astype(jnp.bfloat16)

    def z_copy(t, i):
        sh, f0, nf = CHUNKS[t]
        target = (z + i) % 8
        keep = pltpu.make_async_remote_copy(
            src_ref=white.at[sh, x_lo * 8 + target, pl.ds(f0, nf)],
            dst_ref=bands_ref.at[0, sh, pl.ds(f0, nf), x_lo * 8 + z],
            send_sem=z_send.at[t, 0],
            recv_sem=z_recv.at[t, 0],
            device_id=(chan, x_lo * 8 + target),
            device_id_type=MESH,
        )
        hand = pltpu.make_async_remote_copy(
            src_ref=white.at[sh, (1 - x_lo) * 8 + target, pl.ds(f0, nf)],
            dst_ref=aside.at[sh, pl.ds(f0, nf), z],
            send_sem=z_send.at[t, 1],
            recv_sem=z_recv.at[t, 1],
            device_id=(chan, x_lo * 8 + target),
            device_id_type=MESH,
        )
        return keep, hand

    def local_copy(t):
        sh, f0, nf = CHUNKS[t]
        keep = pltpu.make_async_copy(
            white.at[sh, x_lo * 8 + z, pl.ds(f0, nf)],
            bands_ref.at[0, sh, pl.ds(f0, nf), x_lo * 8 + z],
            z_recv.at[t, 0],
        )
        hand = pltpu.make_async_copy(
            white.at[sh, (1 - x_lo) * 8 + z, pl.ds(f0, nf)],
            aside.at[sh, pl.ds(f0, nf), z],
            z_recv.at[t, 1],
        )
        return keep, hand

    def z_wait(t):
        sh, f0, nf = CHUNKS[t]
        keep = bands_ref.at[0, sh, pl.ds(f0, nf), pl.ds(x_lo * 8, 8)]
        hand = aside.at[sh, pl.ds(f0, nf)]
        pltpu.make_async_copy(keep, keep, z_recv.at[t, 0]).wait()
        pltpu.make_async_copy(hand, hand, z_recv.at[t, 1]).wait()

    def z_done(t):
        sh, f0, nf = CHUNKS[t]
        sent = aside.at[sh, pl.ds(f0, nf), pl.ds(0, 7)]
        pltpu.make_async_copy(sent, sent, z_send.at[t, 0]).wait()
        pltpu.make_async_copy(sent, sent, z_send.at[t, 1]).wait()

    def send_chunk(t):
        def one(i):
            for copy in z_copy(t, i):
                copy.start()

        each(1, 8, one)
        for copy in local_copy(t):
            copy.start()

    def part_of(slot, t, side):
        sh, f0, nf = CHUNKS[t]
        return bands_ref.at[slot, sh, pl.ds(f0, nf), pl.ds(side * 8, 8)]

    def block_copy(source, slot, send, target, t, side, part):
        return pltpu.make_async_remote_copy(
            src_ref=part_of(source, t, side),
            dst_ref=part_of(slot, t, side),
            send_sem=send.at[t, part],
            recv_sem=slot_recv.at[slot, t, part],
            device_id=(target, seg),
            device_id_type=MESH,
        )

    def aside_copy(t, slot, send, recv, target):
        sh, f0, nf = CHUNKS[t]
        return pltpu.make_async_remote_copy(
            src_ref=aside.at[sh, pl.ds(f0, nf)],
            dst_ref=part_of(slot, t, x_lo),
            send_sem=send,
            recv_sem=recv,
            device_id=(target, (1 - x_lo) * 8 + z),
            device_id_type=MESH,
        )

    def side_of(part):
        return x_lo if part == 0 else 1 - x_lo

    def pass_copy(t):
        return aside_copy(t, 0, pass_send.at[t], pass_recv.at[t], chan)

    def cross_own(t):
        return block_copy(0, 2, cross_send, chan // 4 * 4 + core, t, x_lo, 0)

    def cross_other(t):
        return aside_copy(
            t, 2, cross_send.at[t, 1], slot_recv.at[2, t, 1], chan // 4 * 4 + core
        )

    def down_copy(t, part):
        return block_copy(0, 4, y_send, (chan + 12) % 16, t, side_of(part), part)

    def aside_down(t):
        sh, f0, nf = CHUNKS[t]
        return pltpu.make_async_remote_copy(
            src_ref=aside.at[sh, pl.ds(f0, nf)],
            dst_ref=far_aside.at[sh, pl.ds(f0, nf)],
            send_sem=aside_send.at[t],
            recv_sem=aside_recv.at[t],
            device_id=((chan + 12) % 16, seg),
            device_id_type=MESH,
        )

    def forward_copy(t, part):
        sh, f0, nf = CHUNKS[t]
        if part == 1 and t in DIRECT:
            return pltpu.make_async_remote_copy(
                src_ref=far_aside.at[sh, pl.ds(f0, nf)],
                dst_ref=part_of(2, t, x_lo),
                send_sem=x_send.at[t, 1],
                recv_sem=slot_recv.at[2, t, 1],
                device_id=(chan // 4 * 4 + 2 + core, (1 - x_lo) * 8 + z),
                device_id_type=MESH,
            )
        return block_copy(4, 2, x_send, chan // 4 * 4 + 2 + core, t, side_of(part), part)

    other = chan + 1 - 2 * core

    def core_copy(source, slot, t, part):
        send = core_a_send if slot == 1 else core_b_send
        return block_copy(source, slot, send, other, t, side_of(part), part)

    def arrived(slot, t, part):
        block_copy(0, slot, y_send, other, t, side_of(part), part).wait_recv()

    has_near = jnp.logical_or(y < 3, x_hi == 0)
    has_far = y < 3

    def send_own(t, part):
        @pl.when(y > 0)
        def _():
            down_copy(t, part).start()

        @pl.when(core == 1)
        def _():
            core_copy(0, 1, t, part).start()

    def after_z(t):
        z_wait(t)
        pass_copy(t).start()
        send_own(t, 0)
        if t in DIRECT:

            @pl.when(jnp.logical_and(y > 0, x_hi == 0))
            def _():
                aside_down(t).start()

        @pl.when(x_hi == 1)
        def _():
            cross_other(t).start()
            cross_own(t).start()

    def after_pass(t):
        pass_copy(t).wait_recv()
        send_own(t, 1)

    def after_far(t):
        @pl.when(has_far)
        def _():
            for part in range(2):
                if part == 1 and t in DIRECT:

                    @pl.when(x_hi == 0)
                    def _():
                        aside_down(t).wait_recv()
                        forward_copy(t, part).start()

                arrived(4, t, part)

                if part == 0 or t not in DIRECT:

                    @pl.when(x_hi == 0)
                    def _():
                        forward_copy(t, part).start()

                @pl.when(core == 0)
                def _():
                    core_copy(4, 3, t, part).start()

    def after_near(t):
        @pl.when(has_near)
        def _():
            for part in range(2):
                arrived(2, t, part)

                @pl.when(core == 0)
                def _():
                    core_copy(2, 1, t, part).start()

                @pl.when(core == 1)
                def _():
                    core_copy(2, 3, t, part).start()

    def power_copy(i):
        return pltpu.make_async_remote_copy(
            src_ref=power,
            dst_ref=parts.at[chan],
            send_sem=power_send,
            recv_sem=power_recv,
            device_id=((chan + i) % N_CHAN, seg),
            device_id_type=MESH,
        )

    def weight_copy(i):
        return pltpu.make_async_remote_copy(
            src_ref=own_weights,
            dst_ref=weights_ref.at[seg],
            send_sem=weight_send,
            recv_sem=weight_recv,
            device_id=(chan, (seg + i) % N_SEG),
            device_id_type=MESH,
        )

    each(0, HALF // GROUP, whiten_group)
    first = True
    for t, chunk in enumerate(CHUNKS):
        if chunk[0] == 0:
            arrange(*chunk)
            if first:
                pl.semaphore_wait(barrier, 31)
                first = False
            send_chunk(t)
    each(HALF // GROUP, SEG_PAD // GROUP, whiten_group)

    lane = lax.broadcasted_iota(jnp.int32, (SEG_PAD, 1, 128), 2)
    row = lax.broadcasted_iota(jnp.int32, (SEG_PAD, 1, 128), 0)
    totals = jnp.sum(energy[...], axis=2, keepdims=True)
    power[...] = jnp.sum(jnp.where(lane == row, totals, 0.0), axis=0)
    each(1, 16, lambda i: power_copy(i).start())
    for t, chunk in enumerate(CHUNKS):
        if chunk[0] == 1:
            arrange(*chunk)
            send_chunk(t)

    def share_weights():
        parts[chan] = power[...]
        others = parts.at[pl.ds(0, N_CHAN - 1)]
        pltpu.make_async_copy(others, others, power_recv).wait()
        total = jnp.sum(parts[...], axis=0)
        lane = lax.broadcasted_iota(jnp.int32, (1, 128), 1)
        weights = 1.0 / jnp.sqrt(total / (CHANNELS * L) + eps_power)
        weights = jnp.where(lane < SEG_DEV, weights, 0.0)
        own_weights[...] = weights
        weights_ref[seg] = weights
        each(1, 16, lambda i: weight_copy(i).start())

    n = len(CHUNKS)
    for step in range(n + 4):
        if step == 2:
            share_weights()
        if 0 <= step - 1 < n:
            after_pass(step - 1)
        if step < n:
            after_z(step)
        if 0 <= step - 2 < n:
            after_far(step - 2)
        if 0 <= step - 4 < n:
            after_near(step - 4)

    for t in range(n):
        for part in range(2):

            @pl.when(jnp.logical_or(core == 0, has_near))
            def _():
                arrived(1, t, part)

            @pl.when(jnp.logical_or(jnp.logical_and(core == 0, has_near), has_far))
            def _():
                arrived(3, t, part)

    for t in range(n):
        z_done(t)
        pass_copy(t).wait_send()

        @pl.when(x_hi == 1)
        def _():
            cross_other(t).wait_send()
            cross_own(t).wait_send()

        if t in DIRECT:

            @pl.when(jnp.logical_and(y > 0, x_hi == 0))
            def _():
                aside_down(t).wait_send()

        for part in range(2):

            @pl.when(y > 0)
            def _():
                down_copy(t, part).wait_send()

            @pl.when(jnp.logical_and(has_far, x_hi == 0))
            def _():
                forward_copy(t, part).wait_send()

            @pl.when(jnp.logical_or(core == 1, has_near))
            def _():
                core_copy(0, 1, t, part).wait_send()

            @pl.when(
                jnp.logical_or(
                    jnp.logical_and(core == 1, has_near), jnp.logical_and(core == 0, has_far)
                )
            )
            def _():
                core_copy(0, 3, t, part).wait_send()

    others = weights_ref.at[pl.ds(0, N_SEG - 1)]
    for sem in (power_send, weight_send, weight_recv):
        pltpu.make_async_copy(others, others, sem).wait()


def exchange(samples, live):
    dma = pltpu.SemaphoreType.DMA
    n = len(CHUNKS)
    return pl.pallas_call(
        exchange_kernel,
        out_shape=(
            jax.ShapeDtypeStruct((NEAR, 2, BAND, N_SEG, 2 * HALF, CH), jnp.bfloat16),
            jax.ShapeDtypeStruct((N_SEG, 1, 128), jnp.float32),
        ),
        in_specs=[
            pl.BlockSpec(memory_space=pltpu.HBM),
            pl.BlockSpec(memory_space=pltpu.HBM),
            pl.BlockSpec(memory_space=pltpu.HBM),
        ],
        out_specs=(
            pl.BlockSpec(memory_space=pltpu.VMEM),
            pl.BlockSpec(memory_space=pltpu.VMEM),
        ),
        scratch_shapes=[
            pltpu.VMEM((1, CH), jnp.int32),
            pltpu.VMEM((SEG_PAD, CH, L), jnp.bfloat16),
            pltpu.VMEM((L, 2 * F), jnp.bfloat16),
            pltpu.VMEM((CH, 128), jnp.float32),
            pltpu.VMEM((F, CH), jnp.float32),
            pltpu.VMEM((GROUP, F + 16, CH), jnp.float32),
            pltpu.VMEM((SEG_PAD, 1, 128), jnp.float32),
            pltpu.VMEM((2, 2, HALF * 2 * F, 128), jnp.float32),
            pltpu.VMEM((2, N_SEG, BAND, 2 * HALF, CH), jnp.bfloat16),
            pltpu.VMEM((2, BAND, 8, 2 * HALF, CH), jnp.bfloat16),
            pltpu.VMEM((2, BAND, 8, 2 * HALF, CH), jnp.bfloat16),
            pltpu.VMEM((1, 128), jnp.float32),
            pltpu.VMEM((N_CHAN, 1, 128), jnp.float32),
            pltpu.VMEM((1, 128), jnp.float32),
            dma((SEG_DEV,)),
            dma,
            dma,
            dma,
            dma,
            dma,
            dma,
            dma((n, 2)),
            dma((n, 2)),
            dma((n,)),
            dma((n,)),
            dma((n, 2)),
            dma((n, 2)),
            dma((n, 2)),
            dma((n, 2)),
            dma((n, 2)),
            dma((NEAR, n, 2)),
            dma((n,)),
            dma((n,)),
        ],
        compiler_params=pltpu.CompilerParams(
            collective_id=0, has_side_effects=True, vmem_limit_bytes=VMEM_LIMIT
        ),
    )(*[
        pltpu.with_memory_space_constraint(value, pltpu.HBM)
        for value in (samples, jnp.asarray(dft_table()), live)
    ])


def cross_kernel(chan_ref, bands_ref, weights_ref, out_ref, left, result, out_sem):
    lane = lax.broadcasted_iota(jnp.int32, (HALF, 128), 1)
    row = lax.broadcasted_iota(jnp.int32, (HALF, 128), 0)
    factor = math.sqrt(SEGMENTS) / jnp.sum(weights_ref[...])
    block = chan_ref[0]
    mine = lax.broadcasted_iota(jnp.int32, (CH, CH), 0)
    theirs = lax.broadcasted_iota(jnp.int32, (CH, CH), 1)
    for f in range(BAND):
        for sh in range(2):
            for source in range(N_SEG):
                spread = jnp.broadcast_to(weights_ref[source], (HALF, 128))
                scale = jnp.where(lane == row + sh * HALF, spread, 0.0)
                scale = jnp.sum(scale, axis=1, keepdims=True) * factor
                both = bands_ref[0, sh, f, source].astype(jnp.float32)
                real = both[:HALF] * scale
                imag = both[HALF:] * scale
                first = (sh * N_SEG + source) * 2 * HALF
                rows = slice(first, first + 2 * HALF)
                left[f % 2, 0, rows, :] = jnp.concatenate([real, imag], axis=0).astype(jnp.bfloat16)
                left[f % 2, 1, rows, :] = jnp.concatenate([-imag, real], axis=0).astype(jnp.bfloat16)
        turned = [left[f % 2, r].T for r in range(2)]
        for k in range(NEAR):
            for r in range(2):
                product = jnp.zeros((CH, CH), jnp.float32)
                for sh in range(2):
                    partner = bands_ref[k, sh, f].reshape(CH, CH)
                    product += jnp.dot(
                        turned[r][:, sh * CH : (sh + 1) * CH],
                        partner,
                        preferred_element_type=jnp.float32,
                    )
                keep = block + k < N_CHAN
                if k == 0:
                    keep = jnp.logical_and(keep, theirs > mine)
                if k == REACH:
                    keep = jnp.logical_and(keep, theirs <= mine)
                product = jnp.where(keep, product, 0.0)
                result[f, k, :, r * CH : (r + 1) * CH] = product.astype(jnp.bfloat16)
            pltpu.make_async_copy(result.at[f, k], out_ref.at[f, k], out_sem.at[f, k]).start()
    for f in range(BAND):
        for k in range(NEAR):
            pltpu.make_async_copy(result.at[f, k], out_ref.at[f, k], out_sem.at[f, k]).wait()


def cross(chan, bands, weights):
    return pl.pallas_call(
        cross_kernel,
        out_shape=jax.ShapeDtypeStruct((BAND, NEAR, CH, 2 * CH), jnp.bfloat16),
        in_specs=[
            pl.BlockSpec(memory_space=pltpu.SMEM),
            pl.BlockSpec(memory_space=pltpu.VMEM),
            pl.BlockSpec(memory_space=pltpu.VMEM),
        ],
        out_specs=pl.BlockSpec(memory_space=pltpu.HBM),
        scratch_shapes=[
            pltpu.VMEM((2, 2, N_SEG * 2 * SEG_PAD, CH), jnp.bfloat16),
            pltpu.VMEM((BAND, NEAR, CH, 2 * CH), jnp.bfloat16),
            pltpu.SemaphoreType.DMA((BAND, NEAR)),
        ],
        compiler_params=pltpu.CompilerParams(vmem_limit_bytes=40 << 20),
    )(chan, bands, weights)


def on_device(samples, live_trace):
    by_segment = jnp.transpose(samples, (1, 0, 2))
    bands, weights = exchange(by_segment, live_trace.reshape(1, CH))
    chan = lax.axis_index("chan").reshape(1)
    stacked = cross(chan, bands, weights)
    return jnp.transpose(stacked, (0, 2, 1, 3))


def solution(mesh):
    in_specs = (P("chan", "seg", None), P("chan"))
    out_specs = P("seg", "chan", None, None)
    return jax.shard_map(
        on_device, mesh=mesh, in_specs=in_specs, out_specs=out_specs, check_vma=False
    )
```

```python
import functools
import math

import jax
import jax.numpy as jnp
import numpy as np
from jax import lax
from jax.experimental import pallas as pl
from jax.experimental.pallas import tpu as pltpu
from jax.sharding import PartitionSpec as P

L = 1024
F = 64
F0 = 16
REACH = 4
NEAR = 5
CH = 256
CHANNELS = 4096
SEGMENTS = 240
N_CHAN = 16
N_SEG = 16
SEG_DEV = 15
SEG_PAD = 16
HALF = 8
BAND = F // N_SEG
GROUP = 4
DIRECT = (1, 3, 5, 6, 7)
VMEM_LIMIT = 40 << 20
CHUNKS = tuple((t // 4, t % 4, 1) for t in range(8))

eps_power = 1e-06
water_level = 0.1
smooth_half = 2

MESH = pl.DeviceIdType.MESH


def dft_table():
    time_index = np.arange(L)
    bin_number = np.arange(F) + F0
    phase_step = (time_index[:, None] * bin_number[None, :] % L).astype(np.float32)
    angle = phase_step * np.float32(2.0 * math.pi / L)
    taper = np.float32(0.5) - np.float32(0.5) * np.cos(
        time_index.astype(np.float32) * np.float32(2.0 * math.pi / L)
    )
    real = taper[:, None] * np.cos(angle)
    imag = -taper[:, None] * np.sin(angle)
    return np.concatenate([real, imag], axis=1).astype(jnp.bfloat16)


def each(first, last, fn):
    def step(i, carry):
        fn(i)
        return carry

    lax.fori_loop(first, last, step, 0)


def exchange_kernel(
    samples_ref,
    table_hbm,
    live_hbm,
    bands_ref,
    weights_ref,
    live_ref,
    samples,
    table,
    live_column,
    inverse,
    padded,
    energy,
    wide,
    white,
    aside,
    far_aside,
    power,
    parts,
    own_weights,
    load_sem,
    table_sem,
    live_sem,
    power_send,
    power_recv,
    weight_send,
    weight_recv,
    z_send,
    z_recv,
    pass_send,
    pass_recv,
    y_send,
    x_send,
    cross_send,
    core_a_send,
    core_b_send,
    slot_recv,
    aside_send,
    aside_recv,
):
    chan = lax.axis_index("chan")
    seg = lax.axis_index("seg")
    y = chan // 4
    x_hi = (chan // 2) % 2
    core = chan % 2
    x_lo = seg // 8
    z = seg % 8

    def load(j):
        return pltpu.make_async_copy(samples_ref.at[j], samples.at[j], load_sem.at[j])

    load_table = pltpu.make_async_copy(table_hbm, table, table_sem)
    load_live = pltpu.make_async_copy(live_hbm, live_ref, live_sem)
    load_live.start()
    load_table.start()
    each(0, SEG_DEV, lambda j: load(j).start())

    barrier = pltpu.get_barrier_semaphore()

    def greet(i):
        pl.semaphore_signal(
            barrier, inc=1, device_id=(chan, (seg + i) % N_SEG), device_id_type=MESH
        )
        pl.semaphore_signal(
            barrier, inc=1, device_id=((chan + i) % N_CHAN, seg), device_id_type=MESH
        )

    each(1, 16, greet)
    pl.semaphore_signal(
        barrier,
        inc=1,
        device_id=(chan + 2 - 4 * x_hi, (1 - x_lo) * 8 + z),
        device_id_type=MESH,
    )

    load_live.wait()
    live_row = live_ref[...].astype(jnp.float32)
    live_column[...] = jnp.broadcast_to(live_row, (128, CH)).T
    bins = lax.broadcasted_iota(jnp.int32, (F, CH), 0)
    count = jnp.minimum(bins, smooth_half) + jnp.minimum(F - 1 - bins, smooth_half) + 1
    inverse[...] = 1.0 / count.astype(jnp.float32)
    padded[...] = jnp.zeros_like(padded)
    samples[SEG_DEV] = jnp.zeros((CH, L), jnp.bfloat16)
    load_table.wait()

    def whiten(j, slot):
        x = samples[j]
        spectra = jnp.dot(x, table[...], preferred_element_type=jnp.float32)
        squares = jnp.zeros((CH, 128), jnp.float32)
        for tile in range(L // 128):
            part = x[:, tile * 128 : (tile + 1) * 128].astype(jnp.float32)
            squares += part * part
        energy[j] = jnp.sum(squares * live_column[...], axis=0, keepdims=True)
        spectra = spectra.T
        real = spectra[:F]
        imag = spectra[F:]
        level = real * real + imag * imag
        padded[slot, 8 : 8 + F, :] = level
        near = level
        for distance in (-2, -1, 1, 2):
            near += padded[slot, 8 + distance : 8 + distance + F, :]
        mean = jnp.sum(level, axis=0, keepdims=True) * (water_level / F)
        gain = live_row / jnp.sqrt(near * inverse[...] + mean + eps_power)
        real = real * gain
        imag = imag * gain
        base = pl.multiple_of((j % HALF) * 2 * F, 2 * F)
        for half in range(2):
            lanes = slice(half * 128, half * 128 + 128)
            wide[j // HALF, half, pl.ds(base, F), :] = real[:, lanes]
            wide[j // HALF, half, pl.ds(base + F, F), :] = imag[:, lanes]

    def whiten_group(i):
        for slot in range(GROUP - 1):
            load(GROUP * i + slot).wait()

        @pl.when(GROUP * i + GROUP - 1 < SEG_DEV)
        def _():
            load(GROUP * i + GROUP - 1).wait()

        for slot in range(GROUP):
            whiten(GROUP * i + slot, slot)

    def arrange(sh, f0, nf):
        for f in range(f0, f0 + nf):
            for band in range(N_SEG):
                for half in range(2):
                    rows = [
                        wide[sh, half, pl.ds(r * F + band * BAND + f, HALF, stride=2 * F), :]
                        for r in range(2)
                    ]
                    white[sh, band, f, :, half * 128 : half * 128 + 128] = jnp.concatenate(
                        rows, axis=0
                    ).astype(jnp.bfloat16)

    def z_copy(t, i):
        sh, f0, nf = CHUNKS[t]
        target = (z + i) % 8
        keep = pltpu.make_async_remote_copy(
            src_ref=white.at[sh, x_lo * 8 + target, pl.ds(f0, nf)],
            dst_ref=bands_ref.at[0, sh, pl.ds(f0, nf), x_lo * 8 + z],
            send_sem=z_send.at[t, 0],
            recv_sem=z_recv.at[t, 0],
            device_id=(chan, x_lo * 8 + target),
            device_id_type=MESH,
        )
        hand = pltpu.make_async_remote_copy(
            src_ref=white.at[sh, (1 - x_lo) * 8 + target, pl.ds(f0, nf)],
            dst_ref=aside.at[sh, pl.ds(f0, nf), z],
            send_sem=z_send.at[t, 1],
            recv_sem=z_recv.at[t, 1],
            device_id=(chan, x_lo * 8 + target),
            device_id_type=MESH,
        )
        return keep, hand

    def local_copy(t):
        sh, f0, nf = CHUNKS[t]
        keep = pltpu.make_async_copy(
            white.at[sh, x_lo * 8 + z, pl.ds(f0, nf)],
            bands_ref.at[0, sh, pl.ds(f0, nf), x_lo * 8 + z],
            z_recv.at[t, 0],
        )
        hand = pltpu.make_async_copy(
            white.at[sh, (1 - x_lo) * 8 + z, pl.ds(f0, nf)],
            aside.at[sh, pl.ds(f0, nf), z],
            z_recv.at[t, 1],
        )
        return keep, hand

    def z_wait(t):
        sh, f0, nf = CHUNKS[t]
        keep = bands_ref.at[0, sh, pl.ds(f0, nf), pl.ds(x_lo * 8, 8)]
        hand = aside.at[sh, pl.ds(f0, nf)]
        pltpu.make_async_copy(keep, keep, z_recv.at[t, 0]).wait()
        pltpu.make_async_copy(hand, hand, z_recv.at[t, 1]).wait()

    def z_done(t):
        sh, f0, nf = CHUNKS[t]
        sent = aside.at[sh, pl.ds(f0, nf), pl.ds(0, 7)]
        pltpu.make_async_copy(sent, sent, z_send.at[t, 0]).wait()
        pltpu.make_async_copy(sent, sent, z_send.at[t, 1]).wait()

    def send_chunk(t):
        def one(i):
            for copy in z_copy(t, i):
                copy.start()

        each(1, 8, one)
        for copy in local_copy(t):
            copy.start()

    def part_of(slot, t, side):
        sh, f0, nf = CHUNKS[t]
        return bands_ref.at[slot, sh, pl.ds(f0, nf), pl.ds(side * 8, 8)]

    def block_copy(source, slot, send, target, t, side, part):
        return pltpu.make_async_remote_copy(
            src_ref=part_of(source, t, side),
            dst_ref=part_of(slot, t, side),
            send_sem=send.at[t, part],
            recv_sem=slot_recv.at[slot, t, part],
            device_id=(target, seg),
            device_id_type=MESH,
        )

    def aside_copy(t, slot, send, recv, target):
        sh, f0, nf = CHUNKS[t]
        return pltpu.make_async_remote_copy(
            src_ref=aside.at[sh, pl.ds(f0, nf)],
            dst_ref=part_of(slot, t, x_lo),
            send_sem=send,
            recv_sem=recv,
            device_id=(target, (1 - x_lo) * 8 + z),
            device_id_type=MESH,
        )

    def side_of(part):
        return x_lo if part == 0 else 1 - x_lo

    def pass_copy(t):
        return aside_copy(t, 0, pass_send.at[t], pass_recv.at[t], chan)

    def cross_own(t):
        return block_copy(0, 2, cross_send, chan // 4 * 4 + core, t, x_lo, 0)

    def cross_other(t):
        return aside_copy(
            t, 2, cross_send.at[t, 1], slot_recv.at[2, t, 1], chan // 4 * 4 + core
        )

    def down_copy(t, part):
        return block_copy(0, 4, y_send, (chan + 12) % 16, t, side_of(part), part)

    def aside_down(t):
        sh, f0, nf = CHUNKS[t]
        return pltpu.make_async_remote_copy(
            src_ref=aside.at[sh, pl.ds(f0, nf)],
            dst_ref=far_aside.at[sh, pl.ds(f0, nf)],
            send_sem=aside_send.at[t],
            recv_sem=aside_recv.at[t],
            device_id=((chan + 12) % 16, seg),
            device_id_type=MESH,
        )

    def forward_copy(t, part):
        sh, f0, nf = CHUNKS[t]
        if part == 1 and t in DIRECT:
            return pltpu.make_async_remote_copy(
                src_ref=far_aside.at[sh, pl.ds(f0, nf)],
                dst_ref=part_of(2, t, x_lo),
                send_sem=x_send.at[t, 1],
                recv_sem=slot_recv.at[2, t, 1],
                device_id=(chan // 4 * 4 + 2 + core, (1 - x_lo) * 8 + z),
                device_id_type=MESH,
            )
        return block_copy(4, 2, x_send, chan // 4 * 4 + 2 + core, t, side_of(part), part)

    other = chan + 1 - 2 * core

    def core_copy(source, slot, t, part):
        send = core_a_send if slot == 1 else core_b_send
        return block_copy(source, slot, send, other, t, side_of(part), part)

    def arrived(slot, t, part):
        block_copy(0, slot, y_send, other, t, side_of(part), part).wait_recv()

    has_near = jnp.logical_or(y < 3, x_hi == 0)
    has_far = y < 3

    def send_own(t, part):
        @pl.when(y > 0)
        def _():
            down_copy(t, part).start()

        @pl.when(core == 1)
        def _():
            core_copy(0, 1, t, part).start()

    def after_z(t):
        z_wait(t)
        pass_copy(t).start()
        send_own(t, 0)
        if t in DIRECT:

            @pl.when(jnp.logical_and(y > 0, x_hi == 0))
            def _():
                aside_down(t).start()

        @pl.when(x_hi == 1)
        def _():
            cross_other(t).start()
            cross_own(t).start()

    def after_pass(t):
        pass_copy(t).wait_recv()
        send_own(t, 1)

    def after_far(t):
        @pl.when(has_far)
        def _():
            for part in range(2):
                if part == 1 and t in DIRECT:

                    @pl.when(x_hi == 0)
                    def _():
                        aside_down(t).wait_recv()
                        forward_copy(t, part).start()

                arrived(4, t, part)

                if part == 0 or t not in DIRECT:

                    @pl.when(x_hi == 0)
                    def _():
                        forward_copy(t, part).start()

                @pl.when(core == 0)
                def _():
                    core_copy(4, 3, t, part).start()

    def after_near(t):
        @pl.when(has_near)
        def _():
            for part in range(2):
                arrived(2, t, part)

                @pl.when(core == 0)
                def _():
                    core_copy(2, 1, t, part).start()

                @pl.when(core == 1)
                def _():
                    core_copy(2, 3, t, part).start()

    def power_copy(i):
        return pltpu.make_async_remote_copy(
            src_ref=power,
            dst_ref=parts.at[chan],
            send_sem=power_send,
            recv_sem=power_recv,
            device_id=((chan + i) % N_CHAN, seg),
            device_id_type=MESH,
        )

    def weight_copy(i):
        return pltpu.make_async_remote_copy(
            src_ref=own_weights,
            dst_ref=weights_ref.at[seg],
            send_sem=weight_send,
            recv_sem=weight_recv,
            device_id=(chan, (seg + i) % N_SEG),
            device_id_type=MESH,
        )

    each(0, HALF // GROUP, whiten_group)
    first = True
    for t, chunk in enumerate(CHUNKS):
        if chunk[0] == 0:
            arrange(*chunk)
            if first:
                pl.semaphore_wait(barrier, 31)
                first = False
            send_chunk(t)
    each(HALF // GROUP, SEG_PAD // GROUP, whiten_group)

    lane = lax.broadcasted_iota(jnp.int32, (SEG_PAD, 1, 128), 2)
    row = lax.broadcasted_iota(jnp.int32, (SEG_PAD, 1, 128), 0)
    totals = jnp.sum(energy[...], axis=2, keepdims=True)
    power[...] = jnp.sum(jnp.where(lane == row, totals, 0.0), axis=0)
    each(1, 16, lambda i: power_copy(i).start())
    for t, chunk in enumerate(CHUNKS):
        if chunk[0] == 1:
            arrange(*chunk)
            send_chunk(t)

    def share_weights():
        parts[chan] = power[...]
        others = parts.at[pl.ds(0, N_CHAN - 1)]
        pltpu.make_async_copy(others, others, power_recv).wait()
        total = jnp.sum(parts[...], axis=0)
        lane = lax.broadcasted_iota(jnp.int32, (1, 128), 1)
        weights = 1.0 / jnp.sqrt(total / (CHANNELS * L) + eps_power)
        weights = jnp.where(lane < SEG_DEV, weights, 0.0)
        own_weights[...] = weights
        weights_ref[seg] = weights
        each(1, 16, lambda i: weight_copy(i).start())

    n = len(CHUNKS)
    for step in range(n + 4):
        if step == 2:
            share_weights()
        if 0 <= step - 1 < n:
            after_pass(step - 1)
        if step < n:
            after_z(step)
        if 0 <= step - 2 < n:
            after_far(step - 2)
        if 0 <= step - 4 < n:
            after_near(step - 4)

    for t in range(n):
        for part in range(2):

            @pl.when(jnp.logical_or(core == 0, has_near))
            def _():
                arrived(1, t, part)

            @pl.when(jnp.logical_or(jnp.logical_and(core == 0, has_near), has_far))
            def _():
                arrived(3, t, part)

    for t in range(n):
        z_done(t)
        pass_copy(t).wait_send()

        @pl.when(x_hi == 1)
        def _():
            cross_other(t).wait_send()
            cross_own(t).wait_send()

        if t in DIRECT:

            @pl.when(jnp.logical_and(y > 0, x_hi == 0))
            def _():
                aside_down(t).wait_send()

        for part in range(2):

            @pl.when(y > 0)
            def _():
                down_copy(t, part).wait_send()

            @pl.when(jnp.logical_and(has_far, x_hi == 0))
            def _():
                forward_copy(t, part).wait_send()

            @pl.when(jnp.logical_or(core == 1, has_near))
            def _():
                core_copy(0, 1, t, part).wait_send()

            @pl.when(
                jnp.logical_or(
                    jnp.logical_and(core == 1, has_near), jnp.logical_and(core == 0, has_far)
                )
            )
            def _():
                core_copy(0, 3, t, part).wait_send()

    others = weights_ref.at[pl.ds(0, N_SEG - 1)]
    for sem in (power_send, weight_send, weight_recv):
        pltpu.make_async_copy(others, others, sem).wait()


def exchange(samples, live):
    dma = pltpu.SemaphoreType.DMA
    n = len(CHUNKS)
    return pl.pallas_call(
        exchange_kernel,
        out_shape=(
            jax.ShapeDtypeStruct((NEAR, 2, BAND, N_SEG, 2 * HALF, CH), jnp.bfloat16),
            jax.ShapeDtypeStruct((N_SEG, 1, 128), jnp.float32),
        ),
        in_specs=[
            pl.BlockSpec(memory_space=pltpu.HBM),
            pl.BlockSpec(memory_space=pltpu.HBM),
            pl.BlockSpec(memory_space=pltpu.HBM),
        ],
        out_specs=(
            pl.BlockSpec(memory_space=pltpu.VMEM),
            pl.BlockSpec(memory_space=pltpu.VMEM),
        ),
        scratch_shapes=[
            pltpu.VMEM((1, CH), jnp.int32),
            pltpu.VMEM((SEG_PAD, CH, L), jnp.bfloat16),
            pltpu.VMEM((L, 2 * F), jnp.bfloat16),
            pltpu.VMEM((CH, 128), jnp.float32),
            pltpu.VMEM((F, CH), jnp.float32),
            pltpu.VMEM((GROUP, F + 16, CH), jnp.float32),
            pltpu.VMEM((SEG_PAD, 1, 128), jnp.float32),
            pltpu.VMEM((2, 2, HALF * 2 * F, 128), jnp.float32),
            pltpu.VMEM((2, N_SEG, BAND, 2 * HALF, CH), jnp.bfloat16),
            pltpu.VMEM((2, BAND, 8, 2 * HALF, CH), jnp.bfloat16),
            pltpu.VMEM((2, BAND, 8, 2 * HALF, CH), jnp.bfloat16),
            pltpu.VMEM((1, 128), jnp.float32),
            pltpu.VMEM((N_CHAN, 1, 128), jnp.float32),
            pltpu.VMEM((1, 128), jnp.float32),
            dma((SEG_DEV,)),
            dma,
            dma,
            dma,
            dma,
            dma,
            dma,
            dma((n, 2)),
            dma((n, 2)),
            dma((n,)),
            dma((n,)),
            dma((n, 2)),
            dma((n, 2)),
            dma((n, 2)),
            dma((n, 2)),
            dma((n, 2)),
            dma((NEAR, n, 2)),
            dma((n,)),
            dma((n,)),
        ],
        compiler_params=pltpu.CompilerParams(
            collective_id=0, has_side_effects=True, vmem_limit_bytes=VMEM_LIMIT
        ),
    )(*[
        pltpu.with_memory_space_constraint(value, pltpu.HBM)
        for value in (samples, jnp.asarray(dft_table()), live)
    ])


def cross_kernel(chan_ref, bands_ref, weights_ref, out_ref, left, result, out_sem):
    lane = lax.broadcasted_iota(jnp.int32, (HALF, 128), 1)
    row = lax.broadcasted_iota(jnp.int32, (HALF, 128), 0)
    factor = math.sqrt(SEGMENTS) / jnp.sum(weights_ref[...])
    scales = [[], []]
    for sh in range(2):
        for source in range(N_SEG):
            spread = jnp.broadcast_to(weights_ref[source] * factor, (HALF, 128))
            scale = jnp.where(lane == row + sh * HALF, spread, 0.0)
            scale = jnp.broadcast_to(jnp.sum(scale, axis=1, keepdims=True), (HALF, CH))
            scales[sh].append(scale)
    block = chan_ref[0]
    mine = lax.broadcasted_iota(jnp.int32, (CH, CH), 0)
    theirs = lax.broadcasted_iota(jnp.int32, (CH, CH), 1)
    for f in range(BAND):
        for sh in range(2):
            for source in range(N_SEG):
                scale = scales[sh][source]
                both = bands_ref[0, sh, f, source].astype(jnp.float32)
                real = both[:HALF] * scale
                imag = both[HALF:] * scale
                first = (sh * N_SEG + source) * 2 * HALF
                rows = slice(first, first + 2 * HALF)
                left[f % 2, 0, rows, :] = jnp.concatenate([real, imag], axis=0).astype(jnp.bfloat16)
                left[f % 2, 1, rows, :] = jnp.concatenate([-imag, real], axis=0).astype(jnp.bfloat16)
        turned = [left[f % 2, r].T for r in range(2)]
        for k in range(NEAR):
            for r in range(2):
                product = jnp.zeros((CH, CH), jnp.float32)
                for sh in range(2):
                    partner = bands_ref[k, sh, f].reshape(CH, CH)
                    product += jnp.dot(
                        turned[r][:, sh * CH : (sh + 1) * CH],
                        partner,
                        preferred_element_type=jnp.float32,
                    )
                keep = block + k < N_CHAN
                if k == 0:
                    keep = jnp.logical_and(keep, theirs > mine)
                if k == REACH:
                    keep = jnp.logical_and(keep, theirs <= mine)
                product = jnp.where(keep, product, 0.0)
                result[f, k, :, r * CH : (r + 1) * CH] = product.astype(jnp.bfloat16)
            pltpu.make_async_copy(result.at[f, k], out_ref.at[f, k], out_sem.at[f, k]).start()
    for f in range(BAND):
        for k in range(NEAR):
            pltpu.make_async_copy(result.at[f, k], out_ref.at[f, k], out_sem.at[f, k]).wait()


def cross(chan, bands, weights):
    return pl.pallas_call(
        cross_kernel,
        out_shape=jax.ShapeDtypeStruct((BAND, NEAR, CH, 2 * CH), jnp.bfloat16),
        in_specs=[
            pl.BlockSpec(memory_space=pltpu.SMEM),
            pl.BlockSpec(memory_space=pltpu.VMEM),
            pl.BlockSpec(memory_space=pltpu.VMEM),
        ],
        out_specs=pl.BlockSpec(memory_space=pltpu.HBM),
        scratch_shapes=[
            pltpu.VMEM((2, 2, N_SEG * 2 * SEG_PAD, CH), jnp.bfloat16),
            pltpu.VMEM((BAND, NEAR, CH, 2 * CH), jnp.bfloat16),
            pltpu.SemaphoreType.DMA((BAND, NEAR)),
        ],
        compiler_params=pltpu.CompilerParams(vmem_limit_bytes=40 << 20),
    )(chan, bands, weights)


def on_device(samples, live_trace):
    by_segment = jnp.transpose(samples, (1, 0, 2))
    bands, weights = exchange(by_segment, live_trace.reshape(1, CH))
    chan = lax.axis_index("chan").reshape(1)
    stacked = cross(chan, bands, weights)
    return jnp.transpose(stacked, (0, 2, 1, 3))


def solution(mesh):
    in_specs = (P("chan", "seg", None), P("chan"))
    out_specs = P("seg", "chan", None, None)
    return jax.shard_map(
        on_device, mesh=mesh, in_specs=in_specs, out_specs=out_specs, check_vma=False
    )
```
